32 devices in a mesh: grp: 4 (over x, core), seq: 8 (over z, y).
Axes of the slice: x: 2, y: 2, z: 4, core: 2. Of those that a mesh axis runs over, the one named last changes fastest.
Arguments:
- queries: bfloat16 [4096, 4096], P(('grp', 'seq')), may hold values from -6 to 6
- kv_pairs: bfloat16 [2, 4096, 256], P(None, ('grp', 'seq')), may hold values from -6 to 6
- residual: bfloat16 [4096, 4096], P(('grp', 'seq')), may hold values from -30 to 30
- norm_gain: bfloat16 [4096], replicated, may hold values from 0.099609375 to 1.8984375
- o_weight: bfloat16 [4096, 4096], P('seq'), may hold values from -0.09375 to 0.09375
- w_in: bfloat16 [32, 4096, 1536], P(('grp', 'seq')), may hold values from -0.09375 to 0.09375
- w_down: bfloat16 [32, 768, 4096], P(('grp', 'seq')), may hold values from -0.21875 to 0.21875
- expert_ids: int32 [4096, 4], P(('grp', 'seq')), may hold values from 0 to 31, all different within a row; in each aligned block of 128 rows (0 to 127, 128 to 255, ...) at most 32 rows name the same one
- route_weights: float32 [4096, 4], P(('grp', 'seq')), may hold values from 0.1 to 0.6
Outputs:
- layer_out: bfloat16 [4096, 4096], P(('grp', 'seq'))
The draws below stay inside these ranges and needn't reach their ends.
Inputs may be any that keep to these rules, and one draw needn't show every extreme that they name: `expert_ids`: within the rows of one device (aligned blocks of 128 rows) no expert is named by more than 32 rows, a bound that some block reaches; each row names 4 different experts, and every expert is named somewhere.
All inputs are finite; a program needn't handle non-finite values.
Results may differ from the reference program's by a relative error of at most 0.01.
Values may be sent and summed in bfloat16 or wider, within the bound.
A program may use at most 128 MiB of HBM per device.

```python
import math
import jax
import jax.numpy as jnp
import numpy as np
from jax import lax

D = 4096
HEADS = 32
KVH = 2
HD = 128
FFE = 768
TOPK = 4
TOK_DEV = 128
EXPERTS = 32
CAP = 32
SEQ_LEN = 1024
TOKENS = 4096
HPD = 4
GROUP = 16
N_GRP = 4
N_SEQ = 8


def draw_queries(key, part):
    base = jnp.clip(jax.random.normal(jax.random.fold_in(key, 11), (TOKENS, HEADS, HD), jnp.float32), -5.5, 5.5)
    return base.reshape(TOKENS, HEADS * HD).astype(jnp.bfloat16)


def draw_kv_pairs(key, part):
    keys_part = jnp.clip(jax.random.normal(jax.random.fold_in(key, 21), (TOKENS, KVH, HD), jnp.float32), -5.5, 5.5)
    values_part = jnp.clip(jax.random.normal(jax.random.fold_in(key, 22), (TOKENS, KVH, HD), jnp.float32), -5.5, 5.5)
    stacked = jnp.stack([keys_part, values_part])
    return stacked.reshape(2, TOKENS, KVH * HD).astype(jnp.bfloat16)


def draw_residual(key, part):
    row_scale = jnp.exp(jax.random.uniform(jax.random.fold_in(key, 31), (TOKENS, 1), jnp.float32, math.log(0.3), math.log(3.0)))
    col_scale = jnp.exp(jax.random.uniform(jax.random.fold_in(key, 32), (1, D), jnp.float32, math.log(0.5), math.log(2.0)))
    base = jnp.clip(jax.random.normal(jax.random.fold_in(key, 33), (TOKENS, D), jnp.float32), -4.0, 4.0)
    return (base * row_scale * col_scale).astype(jnp.bfloat16)


def shard_levels(rng, extent, shards, least, high):
    level, own = 1.0, jax.random.fold_in(rng, 6)
    for axis_at, parts in shards:
        heights = jnp.exp(jax.random.uniform(jax.random.fold_in(own, axis_at), (parts,), jnp.float32, least / len(shards), high / len(shards)))
        level = level * jnp.repeat(heights, extent[axis_at] // parts).reshape([-1 if axis == axis_at else 1 for axis in range(len(extent))])
    return level


def shared_out(rng, own, number, rows, number_of, top, most, lean):
    sequence = jax.random.permutation(rng, number_of)
    heavy_load, usual = load_shares(number_of, rows * top, most, lean, True), load_shares(number_of, rows * top, most, lean, False)
    places = jnp.arange(number_of)

    def named(tallies, turn):
        used = int((tallies > 0).sum())
        fixed = max(1, used // 4)
        passed = fixed + (places - fixed + turn * (used - fixed)) % max(1, number_of - fixed)
        return jnp.zeros((number_of,), jnp.int32).at[sequence[jnp.where(places < fixed, places, passed)]].set(jnp.asarray(tallies, jnp.int32))

    tallies = jnp.where(number % 4 == 0, named(heavy_load, number // 4), named(usual, number - number // 4 - 1))
    mixed = jax.random.permutation(jax.random.fold_in(own, 3), number_of)
    source_of, receiver = mixed[0:number_of // 2 * 2:2], mixed[1:number_of // 2 * 2:2]
    room = jnp.minimum(tallies[source_of] - 1, most - tallies[receiver]) // 2
    room = jnp.where((source_of == sequence[0]) | (receiver == sequence[0]) | (tallies[receiver] == 0), 0, jnp.maximum(room, 0))
    passed = jax.random.randint(jax.random.fold_in(own, 4), (number_of // 2,), 0, 1 << 20) % (room + 1)
    tallies = tallies.at[source_of].add(-passed).at[receiver].add(passed)
    members = jnp.searchsorted(jnp.cumsum(tallies), jnp.arange(rows * top), side="right").astype(jnp.int32)
    table = members.reshape(top, rows).T
    table = table[jax.random.permutation(jax.random.fold_in(own, 1), rows)]
    turn = jax.random.randint(jax.random.fold_in(own, 2), (rows, 1), 0, top)
    return jnp.take_along_axis(table, (jnp.arange(top)[None, :] + turn) % top, axis=1)


def load_shares(count, total, bound, slope, full):
    weights = [(1 << 20) // math.isqrt(rank ** slope) + 1 for rank in range(1, count + 1)]
    largest = bound if full else min(bound, max(-(-total // count), total * weights[0] // sum(weights)))
    least = 1 if total - largest >= count - 1 else 0
    holding, spare = [largest] + [least] * (count - 1), total - largest - least * (count - 1)
    while spare > 0:
        candidates = [i for i in range(1, count) if holding[i] < largest] or [i for i in range(1, count) if holding[i] < bound]
        pool, budget = sum([weights[i] for i in candidates]), spare
        for i in candidates:
            more = min(bound - holding[i], max(1, budget * weights[i] // pool), spare)
            holding[i] = holding[i] + more
            spare = spare - more
    return np.array(holding)


def scatter_about(own_key, dims, deviation, reach, cuts=(), held_as=jnp.bfloat16):
    values = jax.random.normal(own_key, dims, jnp.float32) * deviation
    if len(cuts) > 0:
        values = shard_levels(own_key, dims, cuts, -0.22, 0.18) * values
    return jnp.clip(values, min=-reach, max=reach).astype(held_as)


def setup_inputs(seed: int = 0) -> dict:
    seeds = jax.random.split(jax.random.key(seed), 10)
    queries = draw_queries(jax.random.fold_in(seeds[9], 71), 0)
    kv_pairs = draw_kv_pairs(jax.random.fold_in(seeds[9], 71), 0)
    residual = draw_residual(jax.random.fold_in(seeds[9], 71), 0)
    norm_gain = jnp.clip(1.0 + 0.18 * jax.random.normal(seeds[3], (D,), jnp.float32), 0.099609375, 1.8984375).astype(jnp.bfloat16)
    o_weight = scatter_about(seeds[4], (HEADS * HD, D), (HEADS * HD) ** -0.5, 0.09375, ((0, 8),))
    w_in = scatter_about(seeds[5], (EXPERTS, D, 2 * FFE), D ** -0.5, 0.09375, ((0, 32),))
    w_down = scatter_about(seeds[6], (EXPERTS, FFE, D), FFE ** -0.5, 0.21875, ((0, 32),))
    expert_ids_keys = jax.random.split(jax.random.fold_in(seeds[7], 1), TOKENS // TOK_DEV)
    expert_ids_turns = jax.random.permutation(jax.random.fold_in(seeds[7], 3), TOKENS // TOK_DEV)
    expert_ids = jax.vmap(lambda own, number: shared_out(jax.random.fold_in(seeds[7], 2), own, number, TOK_DEV, EXPERTS, TOPK, CAP, 2))(expert_ids_keys, expert_ids_turns).reshape((TOKENS, TOPK))
    route_weights = jnp.clip(0.1 + 0.5 * jax.random.uniform(seeds[8], (TOKENS, TOPK), jnp.float32) ** shard_levels(seeds[8], (TOKENS, TOPK), ((0, 32),), -0.2, 0.2), 0.1, 0.6)
    return {"queries": queries, "kv_pairs": kv_pairs, "residual": residual, "norm_gain": norm_gain, "o_weight": o_weight, "w_in": w_in, "w_down": w_down, "expert_ids": expert_ids, "route_weights": route_weights}


def head_attention(operands):
    query_rows, key_rows, value_rows = operands
    length = query_rows.shape[0]
    scores = jnp.dot(query_rows, key_rows.T, preferred_element_type=jnp.float32) * (1.0 / HD ** 0.5)
    positions = jnp.arange(length, dtype=jnp.int32)
    allowed = positions[None, :] <= positions[:, None]
    scores = jnp.where(allowed, scores, jnp.float32(-1e+30))
    top_score = lax.optimization_barrier(jnp.max(scores, axis=1, keepdims=True))
    weights = jnp.exp(scores - top_score)
    probs = (weights / lax.optimization_barrier(jnp.sum(weights, axis=1, keepdims=True))).astype(jnp.bfloat16)
    return jnp.dot(probs, value_rows, preferred_element_type=jnp.float32).astype(jnp.bfloat16)

def sequence_attention(operands):
    query_seq, key_seq, value_seq, o_blocks = operands
    query_heads = query_seq.reshape(SEQ_LEN, HEADS, HD).transpose(1, 0, 2)
    key_heads = jnp.repeat(key_seq.reshape(SEQ_LEN, KVH, HD).transpose(1, 0, 2), GROUP, axis=0)
    value_heads = jnp.repeat(value_seq.reshape(SEQ_LEN, KVH, HD).transpose(1, 0, 2), GROUP, axis=0)
    attended = lax.map(head_attention, (query_heads, key_heads, value_heads))
    blocks = attended.reshape(N_SEQ, HPD, SEQ_LEN, HD).transpose(0, 2, 1, 3).reshape(N_SEQ, SEQ_LEN, HPD * HD)

    def add_block(total, pair):
        block_rows, block_weight = pair
        partial_j = jnp.dot(block_rows, block_weight, preferred_element_type=jnp.float32).astype(jnp.bfloat16)
        return (total + partial_j.astype(jnp.float32), None)
    total, unused = lax.scan(add_block, jnp.zeros((SEQ_LEN, D), jnp.float32), (blocks, o_blocks))
    return total

def reference(queries, kv_pairs, residual, norm_gain, o_weight, w_in, w_down, expert_ids, route_weights):
    query_seqs = queries.reshape(N_GRP, SEQ_LEN, HEADS * HD)
    key_seqs = kv_pairs[0].reshape(N_GRP, SEQ_LEN, KVH * HD)
    value_seqs = kv_pairs[1].reshape(N_GRP, SEQ_LEN, KVH * HD)
    o_blocks = o_weight.reshape(N_SEQ, HPD * HD, D)
    attn_out = lax.map(lambda trio: sequence_attention((trio[0], trio[1], trio[2], o_blocks)), (query_seqs, key_seqs, value_seqs))
    attn_out = attn_out.reshape(TOKENS, D)
    mixed = residual.astype(jnp.float32) + attn_out
    mean_square = lax.optimization_barrier(jnp.mean(mixed * mixed, axis=1, keepdims=True))
    normed = (mixed * lax.rsqrt(mean_square + 1e-06) * norm_gain.astype(jnp.float32)).astype(jnp.bfloat16)
    flat_ids = expert_ids.reshape(-1)
    flat_weights = route_weights.reshape(-1)
    slots_total = EXPERTS * CAP

    def one_expert(total, operands):
        expert_index, gate_up, down = operands
        chosen = flat_ids == expert_index
        places = jnp.nonzero(chosen, size=slots_total, fill_value=0)[0].astype(jnp.int32)
        count = jnp.sum(chosen.astype(jnp.int32))
        valid = jnp.arange(slots_total, dtype=jnp.int32) < count
        token_rows = (places // TOPK).astype(jnp.int32)
        inputs = normed[token_rows]
        projected = jnp.dot(inputs, gate_up, preferred_element_type=jnp.float32)
        hidden = (jax.nn.silu(projected[:, :FFE]) * projected[:, FFE:]).astype(jnp.bfloat16)
        expert_out = jnp.dot(hidden, down, preferred_element_type=jnp.float32).astype(jnp.bfloat16)
        scaled = expert_out.astype(jnp.float32) * jnp.where(valid, flat_weights[places], jnp.float32(0.0))[:, None]
        return (total.at[token_rows].add(scaled), None)
    combined, unused = lax.scan(one_expert, jnp.zeros((TOKENS, D), jnp.float32), (jnp.arange(EXPERTS, dtype=jnp.int32), w_in, w_down))
    return (mixed + combined).astype(jnp.bfloat16)
```

```python
import jax
import jax.numpy as jnp
from jax import lax
from jax.sharding import Mesh, PartitionSpec as P

HD = 128
PLANE = ("x", "core", "y")


def ring(value, axis):
    n = lax.axis_size(axis)
    return lax.ppermute(value, axis, [(i, (i + 1) % n) for i in range(n)])


def spread(value, axes):
    n = 1
    for axis in axes:
        n *= lax.axis_size(axis)
    return lax.all_to_all(
        jnp.broadcast_to(value[None], (n,) + value.shape), axes, split_axis=0, concat_axis=0, tiled=True
    )


def gathered_weight(o_weight):
    core = lax.axis_index("core")
    rows = o_weight.shape[0] // 2
    half = lax.dynamic_slice_in_dim(o_weight, core * rows, rows, 0)
    shards = [o_weight]
    for _ in range(lax.axis_size("y") - 1):
        half = ring(half, "y")
        other = ring(half, "core")
        first = jnp.where(core == 0, half, other)
        second = jnp.where(core == 0, other, half)
        shards.append(jnp.concatenate([first, second], axis=0))
    return shards


def attention(queries, kv_pairs):
    tok = queries.shape[0]
    nz, ny = lax.axis_size("z"), lax.axis_size("y")
    y = lax.axis_index("y")
    heads = queries.shape[1] // HD
    per_z = heads // nz
    key_heads = kv_pairs.shape[2] // HD
    sharing = heads // key_heads
    mine = lax.all_to_all(
        queries.reshape(tok, nz, per_z * HD).transpose(1, 0, 2), "z", split_axis=0, concat_axis=0, tiled=True
    )
    parts = [
        kv_pairs[:, :, (z * per_z // sharing) * HD : (z * per_z // sharing + 1) * HD] for z in range(nz) for _ in range(ny)
    ]
    kv = lax.all_to_all(jnp.stack(parts), ("z", "y"), split_axis=0, concat_axis=0, tiled=True)
    keys = kv[:, 0].reshape(nz * ny * tok, HD)
    values = kv[:, 1].reshape(nz * ny * tok, HD)
    scale = 1.0 / HD**0.5
    blocks = []
    for b in range(nz):
        length = (b + 1) * ny * tok
        q = mine[b].reshape(tok, per_z, HD)
        scores = jnp.einsum("qhd,kd->hqk", q, keys[:length], preferred_element_type=jnp.float32) * scale
        at = (b * ny + y) * tok + jnp.arange(tok, dtype=jnp.int32)
        allowed = jnp.arange(length, dtype=jnp.int32)[None, :] <= at[:, None]
        scores = jnp.where(allowed[None], scores, jnp.float32(-1e30))
        weights = jnp.exp(scores - jnp.max(scores, axis=2, keepdims=True))
        total = jnp.sum(weights, axis=2, keepdims=True)
        out = jnp.einsum(
            "hqk,kd->hqd", weights.astype(jnp.bfloat16), values[:length], preferred_element_type=jnp.float32
        )
        out = (out / total).astype(jnp.bfloat16)
        blocks.append(out.transpose(1, 0, 2).reshape(tok, per_z * HD))
    return jnp.stack(blocks)


def shards(queries, kv_pairs, residual, norm_gain, o_weight, w_in, w_down, expert_ids, route_weights):
    tok, width = residual.shape
    nx, nz, ny = lax.axis_size("x"), lax.axis_size("z"), lax.axis_size("y")
    z, y = lax.axis_index("z"), lax.axis_index("y")
    devices = nx * 2 * nz * ny
    plane = devices // nz
    top_count = expert_ids.shape[1]
    capacity = 2 * tok * top_count // devices
    ffe = w_down.shape[1]

    routing = spread(
        jnp.concatenate([expert_ids.astype(jnp.float32), route_weights], axis=1), ("z",)
    )
    o_shards = gathered_weight(o_weight)
    attended = attention(queries, kv_pairs)

    depth = o_weight.shape[0]
    acc = None
    for t in range(nz):
        rows = lax.dynamic_index_in_dim(attended, (z + 2 * nz - 1 - t) % nz, 0, keepdims=False)
        part = jnp.zeros((tok, width), jnp.float32)
        for s, shard in enumerate(o_shards):
            columns = lax.dynamic_slice_in_dim(rows, (y + ny - s) % ny * depth, depth, 1)
            part = part + jnp.dot(columns, shard, preferred_element_type=jnp.float32)
        if acc is not None:
            part = part + ring(acc, "z").astype(jnp.float32)
        acc = part.astype(jnp.bfloat16) if t < nz - 1 else part
    mixed = residual.astype(jnp.float32) + acc
    mean_square = jnp.mean(mixed * mixed, axis=1, keepdims=True)
    normed = (mixed * lax.rsqrt(mean_square + 1e-06) * norm_gain.astype(jnp.float32)).astype(jnp.bfloat16)

    number = jnp.arange(plane, dtype=jnp.int32)
    experts = ((number // ny) * nz + z) * ny + number % ny
    before = (jnp.arange(tok)[None, :] < jnp.arange(tok)[:, None]).astype(jnp.bfloat16)
    slots = jnp.arange(capacity, dtype=jnp.float32)

    def tables(s):
        table = lax.dynamic_index_in_dim(routing, (z + nz - s) % nz, 0, keepdims=False)
        hits = table[:, :top_count, None] == experts.astype(jnp.float32)[None, None, :]
        chosen = jnp.any(hits, axis=1)
        weight = jnp.sum(jnp.where(hits, table[:, top_count:, None], 0.0), axis=1)
        rank = jnp.dot(before, chosen.astype(jnp.bfloat16), preferred_element_type=jnp.float32)
        place = chosen[:, :, None] & (rank[:, :, None] == slots[None, None, :])
        send = place.astype(jnp.bfloat16).reshape(tok, plane * capacity)
        back = jnp.where(place, weight[:, :, None], 0.0).astype(jnp.bfloat16).reshape(tok, plane * capacity)
        return send, back

    made = [tables(s) for s in range(nz)]
    block = normed
    produced = []
    for s in range(nz):
        rows = lax.dot_general(
            made[s][0], block, (((0,), (0,)), ((), ())), preferred_element_type=jnp.float32
        ).astype(jnp.bfloat16)
        if s < nz - 1:
            block = ring(block, "z")
        rows = lax.all_to_all(
            rows.reshape(plane, capacity, width), PLANE, split_axis=0, concat_axis=0, tiled=True
        ).reshape(plane * capacity, width)
        projected = jnp.dot(rows, w_in[0], preferred_element_type=jnp.float32)
        hidden = (jax.nn.silu(projected[:, :ffe]) * projected[:, ffe:]).astype(jnp.bfloat16)
        produced.append(jnp.dot(hidden, w_down[0], preferred_element_type=jnp.float32).astype(jnp.bfloat16))

    acc = None
    for t in range(nz):
        s = (t + 1) % nz
        back = lax.all_to_all(
            produced[s].reshape(plane, capacity, width), PLANE, split_axis=0, concat_axis=0, tiled=True
        ).reshape(plane * capacity, width)
        part = jnp.dot(made[s][1], back, preferred_element_type=jnp.float32)
        if acc is not None:
            part = part + ring(acc, "z").astype(jnp.float32)
        acc = part.astype(jnp.bfloat16) if t < nz - 1 else part
    return (mixed + acc).astype(jnp.bfloat16)


def solution(mesh):
    nz = 4
    n_grp, n_seq = mesh.shape["grp"], mesh.shape["seq"]
    fine = Mesh(mesh.devices.reshape(n_grp // 2, 2, nz, n_seq // nz), ("x", "core", "z", "y"))
    every = ("x", "core", "z", "y")
    return jax.shard_map(
        shards,
        mesh=fine,
        in_specs=(
            P(every, None),
            P(None, every, None),
            P(every, None),
            P(),
            P(("z", "y"), None),
            P(every, None, None),
            P(every, None, None),
            P(every, None),
            P(every, None),
        ),
        out_specs=P(every, None),
        check_vma=False,
    )
```

```python
import jax
import jax.numpy as jnp
from jax import lax
from jax.sharding import Mesh, PartitionSpec as P

HD = 128
PLANE = ("x", "core", "y")


def ring(value, axis):
    n = lax.axis_size(axis)
    return lax.ppermute(value, axis, [(i, (i + 1) % n) for i in range(n)])


def spread(value, axes):
    n = 1
    for axis in axes:
        n *= lax.axis_size(axis)
    return lax.all_to_all(
        jnp.broadcast_to(value[None], (n,) + value.shape), axes, split_axis=0, concat_axis=0, tiled=True
    )


def gathered_weight(o_weight):
    core = lax.axis_index("core")
    rows = o_weight.shape[0] // 2
    half = lax.dynamic_slice_in_dim(o_weight, core * rows, rows, 0)
    shards = [o_weight]
    for _ in range(lax.axis_size("y") - 1):
        half = ring(half, "y")
        other = ring(half, "core")
        first = jnp.where(core == 0, half, other)
        second = jnp.where(core == 0, other, half)
        shards.append(jnp.concatenate([first, second], axis=0))
    return shards


def attention(queries, kv_pairs):
    tok = queries.shape[0]
    nz, ny = lax.axis_size("z"), lax.axis_size("y")
    y = lax.axis_index("y")
    heads = queries.shape[1] // HD
    per_z = heads // nz
    key_heads = kv_pairs.shape[2] // HD
    mine = lax.all_to_all(
        queries.reshape(tok, nz, per_z * HD).transpose(1, 0, 2), "z", split_axis=0, concat_axis=0, tiled=True
    )
    split = kv_pairs.reshape(2, tok, key_heads, HD).transpose(2, 0, 1, 3)
    parts = jnp.broadcast_to(split[:, None], (key_heads, nz * ny // key_heads, 2, tok, HD))
    kv = lax.all_to_all(
        parts.reshape(nz * ny, 2, tok, HD), ("z", "y"), split_axis=0, concat_axis=0, tiled=True
    )
    keys = kv[:, 0].reshape(nz * ny * tok, HD)
    values = kv[:, 1].reshape(nz * ny * tok, HD)
    scale = 1.0 / HD**0.5
    blocks = []
    for b in range(nz):
        length = (b + 1) * ny * tok
        q = mine[b].reshape(tok, per_z, HD)
        scores = jnp.einsum("qhd,kd->hqk", q, keys[:length], preferred_element_type=jnp.float32) * scale
        at = (b * ny + y) * tok + jnp.arange(tok, dtype=jnp.int32)
        allowed = jnp.arange(length, dtype=jnp.int32)[None, :] <= at[:, None]
        scores = jnp.where(allowed[None], scores, jnp.float32(-1e30))
        weights = jnp.exp(scores - jnp.max(scores, axis=2, keepdims=True))
        total = jnp.sum(weights, axis=2, keepdims=True)
        out = jnp.einsum(
            "hqk,kd->hqd", weights.astype(jnp.bfloat16), values[:length], preferred_element_type=jnp.float32
        )
        out = (out / total).astype(jnp.bfloat16)
        blocks.append(out.transpose(1, 0, 2).reshape(tok, per_z * HD))
    return jnp.stack(blocks)


def shards(queries, kv_pairs, residual, norm_gain, o_weight, w_in, w_down, expert_ids, route_weights):
    tok, width = residual.shape
    nx, nz, ny = lax.axis_size("x"), lax.axis_size("z"), lax.axis_size("y")
    z, y = lax.axis_index("z"), lax.axis_index("y")
    devices = nx * 2 * nz * ny
    plane = devices // nz
    top_count = expert_ids.shape[1]
    capacity = 2 * tok * top_count // devices
    ffe = w_down.shape[1]

    routing = spread(
        jnp.concatenate([expert_ids.astype(jnp.float32), route_weights], axis=1), ("z",)
    )
    o_shards = gathered_weight(o_weight)
    attended = attention(queries, kv_pairs)

    depth = o_weight.shape[0]
    acc = None
    for t in range(nz):
        rows = lax.dynamic_index_in_dim(attended, (z + 2 * nz - 1 - t) % nz, 0, keepdims=False)
        part = jnp.zeros((tok, width), jnp.float32)
        for s, shard in enumerate(o_shards):
            columns = lax.dynamic_slice_in_dim(rows, (y + ny - s) % ny * depth, depth, 1)
            part = part + jnp.dot(columns, shard, preferred_element_type=jnp.float32)
        if acc is not None:
            part = part + ring(acc, "z").astype(jnp.float32)
        acc = part.astype(jnp.bfloat16) if t < nz - 1 else part
    mixed = residual.astype(jnp.float32) + acc
    mean_square = jnp.mean(mixed * mixed, axis=1, keepdims=True)
    normed = (mixed * lax.rsqrt(mean_square + 1e-06) * norm_gain.astype(jnp.float32)).astype(jnp.bfloat16)

    x, core = lax.axis_index("x"), lax.axis_index("core")
    number = jnp.arange(plane, dtype=jnp.int32)
    peer_x = (x + number // (2 * ny)) % nx
    peer_core = (core + number // ny % 2) % 2
    peer_y = (y + number % ny) % ny
    experts = ((peer_x * 2 + peer_core) * nz + z) * ny + peer_y

    def moves(r, sign):
        pairs = []
        for i in range(plane):
            to_x = (i // (2 * ny) + sign * (r // (2 * ny))) % nx
            to_core = (i // ny % 2 + sign * (r // ny % 2)) % 2
            to_y = (i % ny + sign * (r % ny)) % ny
            pairs.append((i, (to_x * 2 + to_core) * ny + to_y))
        return pairs

    before = (jnp.arange(tok)[None, :] < jnp.arange(tok)[:, None]).astype(jnp.bfloat16)
    slots = jnp.arange(capacity, dtype=jnp.float32)

    def tables(s):
        table = lax.dynamic_index_in_dim(routing, (z + nz - s) % nz, 0, keepdims=False)
        hits = table[:, :top_count, None] == experts.astype(jnp.float32)[None, None, :]
        chosen = jnp.any(hits, axis=1)
        weight = jnp.sum(jnp.where(hits, table[:, top_count:, None], 0.0), axis=1)
        rank = jnp.dot(before, chosen.astype(jnp.bfloat16), preferred_element_type=jnp.float32)
        place = chosen[:, :, None] & (rank[:, :, None] == slots[None, None, :])
        send = place.astype(jnp.bfloat16).reshape(tok, plane * capacity)
        back = jnp.where(place, weight[:, :, None], 0.0).astype(jnp.bfloat16).reshape(tok, plane * capacity)
        return send, back

    made = [tables(s) for s in range(nz)]
    def expert(rows):
        projected = jnp.dot(rows, w_in[0], preferred_element_type=jnp.float32)
        hidden = (jax.nn.silu(projected[:, :ffe]) * projected[:, ffe:]).astype(jnp.bfloat16)
        return jnp.dot(hidden, w_down[0], preferred_element_type=jnp.float32).astype(jnp.bfloat16)

    def exchange(rows, sign):
        parts = []
        for r in range(plane):
            part = rows[r * capacity : (r + 1) * capacity]
            parts.append(part if r == 0 else lax.ppermute(part, PLANE, moves(r, sign)))
        return jnp.concatenate(parts, axis=0)

    blocks = [normed]
    for s in range(nz - 1):
        blocks.append(ring(blocks[-1], "z"))
    returned = []
    for s in range(nz):
        rows = lax.dot_general(
            made[s][0], blocks[s], (((0,), (0,)), ((), ())), preferred_element_type=jnp.float32
        ).astype(jnp.bfloat16)
        returned.append(exchange(expert(exchange(rows, 1)), -1))

    acc = None
    for t in range(nz):
        s = (t + 1) % nz
        part = jnp.dot(made[s][1], returned[s], preferred_element_type=jnp.float32)
        if acc is not None:
            part = part + ring(acc, "z").astype(jnp.float32)
        acc = part.astype(jnp.bfloat16) if t < nz - 1 else part
    return (mixed + acc).astype(jnp.bfloat16)


def solution(mesh):
    nz = 4
    n_grp, n_seq = mesh.shape["grp"], mesh.shape["seq"]
    fine = Mesh(mesh.devices.reshape(n_grp // 2, 2, nz, n_seq // nz), ("x", "core", "z", "y"))
    every = ("x", "core", "z", "y")
    return jax.shard_map(
        shards,
        mesh=fine,
        in_specs=(
            P(every, None),
            P(None, every, None),
            P(every, None),
            P(),
            P(("z", "y"), None),
            P(every, None, None),
            P(every, None, None),
            P(every, None),
            P(every, None),
        ),
        out_specs=P(every, None),
        check_vma=False,
    )
```
